1024 devices in a mesh: sect: 8 (over y, core), blk: 32 (over x, z_lo), obs: 4 (over z_hi).
Axes of the slice: x: 4, y: 4, z: 32 (z_hi: 4, z_lo: 8; z = z_hi * 8 + z_lo), core: 2. Of those that a mesh axis runs over, the one named last changes fastest.
Arguments:
- series: float32 [2, 16384, 512], P(None, ('sect', 'blk'), 'obs'), may hold values from -6 to 6
- positions: float32 [3, 16384], P(None, ('sect', 'blk')), may hold values from -1 to 1
- normals: float32 [3, 16384], P(None, ('sect', 'blk')), may hold values from -1 to 1
- areas: float32 [16384], P(('sect', 'blk')), may hold values from 0.3 to 3
- counts: int32 [256], P(('sect', 'blk')), may hold values from 1 to 64, 8192 in all
- observers: float32 [3, 4096], P(None, 'blk'), may hold values from -8 to 8, as said below
Outputs:
- pressure: float32 [2, 64, 4096], P(None, 'obs', 'blk')
The draws below stay inside these ranges and needn't reach their ends.
Inputs may be any that keep to these rules, and one draw needn't show every extreme that they name: The counts over all 256 tiles sum to 8192 and the largest is 64. `observers`: every observer lies between 2 and 8 from the anchor.
All inputs are finite; a program needn't handle non-finite values. No bound on the sum of `counts` on one device may be relied on, other than what follows from the above.
Results may differ from the reference program's by a relative error of at most 0.0003.
Values sent between devices are 32-bit elements; how exact they have to be, the bound alone decides.
No kernel may reach another device: no remote copies, remote signals or barrier semaphores. Data moves between devices by JAX's collectives and lax.ppermute only.
A program may use at most 32 MiB of HBM per device.

```python
import math
import jax
import jax.numpy as jnp
import numpy as np
from jax import lax

SAMPLES = 512
FREQS = 64
P_DEV = 64
TILES = 256
PANELS = 16384
OBSERVERS = 4096


def draw_positions(key, part):
    key_inner, key_sign, key_pick = jax.random.split(key, 3)
    inner = jax.random.uniform(key_inner, (3, PANELS), jnp.float32, -1.0, 1.0)
    toss = jax.random.uniform(key_sign, (3, PANELS), jnp.float32, 0.0, 1.0)
    edge = jnp.where(toss < 0.5, -1.0, 1.0)
    chance = jax.random.uniform(key_pick, (3, PANELS), jnp.float32, 0.0, 1.0)
    share = 1.0 / 3.0
    return jnp.where(chance < share, edge, inner)


def draw_observers(key, part):
    key_radius, key_height, key_angle, key_diag, key_pick = jax.random.split(key, 5)
    radius = jax.random.uniform(key_radius, (OBSERVERS,), jnp.float32, 2.0, 8.0)
    share = 0.125
    height = jax.random.uniform(key_height, (OBSERVERS,), jnp.float32, -1.0, 1.0)
    azimuth = jax.random.uniform(key_angle, (OBSERVERS,), jnp.float32, -math.pi, math.pi)
    across = jnp.sqrt(jnp.maximum(1.0 - height * height, 0.0))
    spread = jnp.stack([radius * across * jnp.cos(azimuth), radius * across * jnp.sin(azimuth), radius * height])
    toss = jax.random.uniform(key_diag, (3, OBSERVERS), jnp.float32, 0.0, 1.0)
    corner = jnp.where(toss < 0.5, -1.0, 1.0) * (2.0 / math.sqrt(3.0))
    chance = jax.random.uniform(key_pick, (OBSERVERS,), jnp.float32, 0.0, 1.0)
    return jnp.where(chance[None, :] < share, corner, spread)


def level_of(rng, dims, cuts, smallest, largest):
    factor_of, own = 1.0, jax.random.fold_in(rng, 6)
    for dim, shards_of in cuts:
        draws = jnp.exp(jax.random.uniform(jax.random.fold_in(own, dim), (shards_of,), jnp.float32, smallest / len(cuts), largest / len(cuts)))
        factor_of = factor_of * jnp.repeat(draws, dims[dim] // shards_of).reshape([-1 if axis == dim else 1 for axis in range(len(dims))])
    return factor_of


def profile(number_of, total, bound, skew):
    loads = [(1 << 20) // math.isqrt(standing ** skew) + 1 for standing in range(2, number_of + 1)]
    rest, given = total - bound - (number_of - 1), [1] * (number_of - 1)
    while rest > 0:
        movable = [i for i in range(number_of - 1) if given[i] < bound]
        mass, remaining = sum([loads[i] for i in movable]), rest
        for i in movable:
            more = min(bound - given[i], max(1, remaining * loads[i] // mass), rest)
            given[i] = given[i] + more
            rest = rest - more
    return np.array([bound] + given)


def ragged_sizes(key, number_of, total, reach, lean):
    if number_of == 2:
        one = jax.random.randint(key, (), max(1, total - reach), min(reach, total - 1) + 1)
        return jnp.stack([one, total - one])
    lengths = jnp.asarray(profile(number_of, total, reach, lean), jnp.int32)
    pairs = (number_of - 1) // 2
    giver, receiver = lengths[1:1 + 2 * pairs:2], lengths[2:2 + 2 * pairs:2]
    margin = jnp.minimum(giver - 1, reach - receiver)
    shifted = jax.random.randint(jax.random.fold_in(key, 1), (pairs,), 0, 1 << 20) % (margin + 1)
    lengths = lengths.at[1:1 + 2 * pairs:2].set(giver - shifted).at[2:2 + 2 * pairs:2].set(receiver + shifted)
    return lengths[jax.random.permutation(jax.random.fold_in(key, 2), number_of)]


def noise(stream_key, dims, scale, most, pieces=(), held_as=jnp.bfloat16):
    array = jax.random.normal(stream_key, dims, jnp.float32) * scale
    if len(pieces) > 0:
        array = level_of(stream_key, dims, pieces, -0.22, 0.18) * array
    return jnp.clip(array, min=-most, max=most).astype(held_as)


def setup_inputs(seed: int = 0) -> dict:
    splits = jax.random.split(jax.random.key(seed), 7)
    return {
        "series": noise(splits[0], (2, PANELS, SAMPLES), 1.0, 6.0, ((1, 256), (2, 4)), jnp.float32),
        "positions": draw_positions(jax.random.fold_in(splits[6], 71), 0),
        "normals": jnp.clip(jax.random.uniform(splits[2], (3, PANELS), jnp.float32, -1.0, 1.0) * level_of(splits[2], (3, PANELS), ((1, 256),), -0.4, 0.0), -1.0, 1.0),
        "areas": jnp.clip(jnp.exp(math.log(3.0) - 2.3025851 * jax.random.uniform(splits[3], (PANELS,), jnp.float32) ** level_of(splits[3], (PANELS,), ((0, 256),), -0.2, 0.2)), 0.3, 3.0),
        "counts": ragged_sizes(splits[4], TILES, TILES * P_DEV // 2, P_DEV, 2).astype(jnp.int32),
        "observers": draw_observers(jax.random.fold_in(splits[6], 71), 0),
    }


WAVE_SCALE = 0.05
FOUR_PI = 4.0 * math.pi

def spectrum(series, frequency_indices, time_steps):
    products = frequency_indices[:, None] * time_steps[None, :] % SAMPLES
    angles = 2.0 * math.pi / SAMPLES * products.astype(jnp.float32)
    dft_scale = SAMPLES ** (-0.5)
    cosines = jnp.cos(angles) * dft_scale
    sines = -jnp.sin(angles) * dft_scale
    real_part = jnp.einsum('ft,cpt->fcp', cosines, series, precision=lax.Precision.HIGHEST)
    imag_part = jnp.einsum('ft,cpt->fcp', sines, series, precision=lax.Precision.HIGHEST)
    return jnp.concatenate([real_part, imag_part], axis=1)

def panel_field(observers, geometry, spectra, wave_numbers):
    offset = observers[:, :, None] - geometry[0][:, None, :]
    radial_separation = jnp.sqrt(lax.optimization_barrier(jnp.sum(offset * offset, axis=0)))
    cosine = lax.optimization_barrier(jnp.sum(geometry[1][:, None, :] * offset, axis=0)) / radial_separation
    spherical_decay = 1.0 / (FOUR_PI * radial_separation)

    def single(element):
        wavenum, emitter_panel = element
        thick_real, load_real, thick_imag, load_imag = (emitter_panel[0], emitter_panel[1], emitter_panel[2], emitter_panel[3])
        phases = wavenum * radial_separation
        cos_phase = jnp.cos(phases)
        sin_phase = jnp.sin(phases)
        amp_real = -wavenum * thick_imag + cosine * (load_real / radial_separation - wavenum * load_imag)
        amp_imag = wavenum * thick_real + cosine * (load_imag / radial_separation + wavenum * load_real)
        out_real = lax.optimization_barrier(jnp.sum(spherical_decay * (cos_phase * amp_real + sin_phase * amp_imag), axis=1))
        out_imag = lax.optimization_barrier(jnp.sum(spherical_decay * (cos_phase * amp_imag - sin_phase * amp_real), axis=1))
        return jnp.stack([out_real, out_imag])
    return lax.map(single, (wave_numbers, jnp.swapaxes(spectra, 0, 1)))

def reference(series, positions, normals, areas, counts, observers):
    slot_index = jnp.arange(PANELS) % P_DEV
    tile_index = jnp.arange(PANELS) // P_DEV
    is_live = slot_index < counts[tile_index]
    weights = areas * is_live.astype(jnp.float32)
    frequency_indices = jnp.arange(FREQS) + 1
    spectra = spectrum(series, frequency_indices, jnp.arange(SAMPLES))
    sources = jnp.swapaxes(spectra, 0, 1) * weights
    geometry = jnp.stack([positions, normals])
    wave_numbers = WAVE_SCALE * frequency_indices.astype(jnp.float32)

    def add_tile(tile_number, pressure_total):
        first_slot = tile_number * P_DEV
        tile_geometry = lax.dynamic_slice_in_dim(geometry, first_slot, P_DEV, 2)
        tile_sources = lax.dynamic_slice_in_dim(sources, first_slot, P_DEV, 2)
        return pressure_total + panel_field(observers, tile_geometry, tile_sources, wave_numbers)
    zeros_start = jnp.zeros((FREQS, 2, OBSERVERS), jnp.float32)
    summed = lax.fori_loop(0, TILES, add_tile, zeros_start)
    return jnp.swapaxes(summed, 0, 1)
```

```python
import math

import jax
import jax.numpy as jnp
import numpy as np
from jax import lax
from jax.experimental import pallas as pl
from jax.experimental.pallas import tpu as pltpu
from jax.sharding import PartitionSpec as P

SAMPLES = 512
FREQS = 64
P_DEV = 64
WAVE_SCALE = 0.05
FOUR_PI = 4.0 * math.pi

PARTS = 4
GROUP = FREQS // PARTS
ROWS = 2 * GROUP
STEPS = SAMPLES // PARTS
RUN = 8
LINES = 4
TILES_HERE = RUN * LINES
CHUNK = ROWS + 8
SECTIONS = 8
LANES = 128
OBS_HERE = 128
VMEM = 48 * 1024 * 1024

ALONG_Z = [[x * RUN + z for z in range(RUN)] for x in range(LINES)]
ALONG_X = [[x * RUN + z for x in range(LINES)] for z in range(RUN)]


def transform_rows():
    out = np.zeros((PARTS, PARTS, ROWS, STEPS), np.float64)
    for part in range(PARTS):
        steps = part * STEPS + np.arange(STEPS)
        for group in range(PARTS):
            bins = group * GROUP + 1 + np.arange(GROUP)
            angle = 2.0 * np.pi * ((bins[:, None] * steps[None, :]) % SAMPLES) / SAMPLES
            out[part, group, :GROUP] = np.cos(angle)
            out[part, group, GROUP:] = -np.sin(angle)
    return (out * SAMPLES**-0.5).astype(np.float32)


def spectrum_kernel(counts, rows, series, positions, normals, areas, keep, send, geometry):
    me = lax.axis_index("obs")
    live = lax.broadcasted_iota(jnp.int32, (1, P_DEV), 1) < counts[0]
    weights = areas[...] * live.astype(jnp.float32)
    weights = jnp.concatenate([weights, weights], axis=1)
    flat = series[...].reshape(2 * P_DEV, STEPS)
    for slot, flip in enumerate((0, 3, 1, 2)):
        spectra = lax.dot_general(
            rows[me, me ^ flip],
            flat,
            (((1,), (1,)), ((), ())),
            precision=lax.Precision.HIGHEST,
            preferred_element_type=jnp.float32,
        )
        target = keep if slot < 2 else send
        target[pl.ds((slot % 2) * ROWS, ROWS), :] = spectra * weights
    geometry[...] = jnp.broadcast_to(counts[0].astype(jnp.float32), (8, LANES))
    geometry[pl.ds(0, 3), :] = jnp.concatenate([positions[...], normals[...]], axis=1)


def spectrum_parts(series, positions, normals, areas, counts):
    block = jax.ShapeDtypeStruct((2 * ROWS, LANES), jnp.float32)
    whole = pl.BlockSpec(memory_space=pltpu.VMEM)
    return pl.pallas_call(
        spectrum_kernel,
        out_shape=(block, block, jax.ShapeDtypeStruct((8, LANES), jnp.float32)),
        in_specs=[pl.BlockSpec(memory_space=pltpu.SMEM)] + [whole] * 5,
        out_specs=(whole,) * 3,
        compiler_params=pltpu.CompilerParams(vmem_limit_bytes=VMEM),
    )(counts, jnp.asarray(transform_rows()), series, positions, normals, areas[None])


BLOCK = 32
SPAN = TILES_HERE * P_DEV // LANES + 1
Q_RE, Q_IM, POS = 0, GROUP, ROWS
L_RE, L_IM, NORMAL = CHUNK, CHUNK + GROUP, CHUNK + ROWS
M_RE, M_IM = 2 * CHUNK, 2 * CHUNK + GROUP
PACKED = 2 * CHUNK + ROWS


def field_kernel(observers, tiles, out, spread, packed, total, final):
    group = lax.axis_index("obs")
    lane = lax.broadcasted_iota(jnp.int32, (CHUNK, LANES), 1)

    def pack(tile, first):
        x = tiles[tile]
        count = tiles[tile, pl.ds(ROWS + 3, 1), pl.ds(0, 1)][0, 0].astype(jnp.int32)
        shift, base = first & (LANES - 1), first >> 7
        ahead = lane >= shift
        for start, x_half, turn in (
            (0, jnp.where(lane < P_DEV, x, 0.0), shift),
            (CHUNK, jnp.where(lane >= P_DEV, x, 0.0), (shift + P_DEV) & (LANES - 1)),
        ):
            turned = pltpu.roll(x_half, turn, 1)
            here = pl.ds(start, CHUNK)
            packed[base, here, :] = jnp.where(ahead, turned, packed[base, here, :])
            packed[base + 1, here, :] = jnp.where(ahead, 0.0, turned)
        return first + count

    live = lax.fori_loop(0, TILES_HERE, pack, jnp.int32(0))
    groups = (live + (LANES - 1)) >> 7

    columns = jnp.transpose(
        jnp.concatenate([observers[...], jnp.zeros((LANES - 3, OBS_HERE), jnp.float32)], axis=0)
    )
    for axis in range(3):
        spread[axis] = jnp.broadcast_to(columns[:, axis : axis + 1], (OBS_HERE, LANES))

    def clear(row, carry):
        total[row] = jnp.zeros((OBS_HERE, LANES), jnp.float32)
        return carry

    lax.fori_loop(0, ROWS, clear, 0)

    numbers = group * GROUP + 1 + lax.broadcasted_iota(jnp.int32, (GROUP, LANES), 0)
    wave = WAVE_SCALE * numbers.astype(jnp.float32)
    odd, high = (group & 1) == 1, (group & 2) == 2

    def panels(at, carry):
        packed[at, pl.ds(M_RE, GROUP), :] = packed[at, pl.ds(L_IM, GROUP), :] / wave
        packed[at, pl.ds(M_IM, GROUP), :] = -packed[at, pl.ds(L_RE, GROUP), :] / wave

        def row(number):
            return jnp.broadcast_to(packed[at, pl.ds(number, 1), :], (BLOCK, LANES))

        def block(step, inner):
            here = pl.ds(pl.multiple_of(step * BLOCK, BLOCK), BLOCK)
            d = [spread[axis, here, :] - row(POS + axis) for axis in range(3)]
            square = d[0] * d[0] + d[1] * d[1] + d[2] * d[2]
            inverse = lax.rsqrt(square)
            inverse = inverse * (1.5 - 0.5 * square * inverse * inverse)
            along = row(NORMAL) * d[0] + row(NORMAL + 1) * d[1] + row(NORMAL + 2) * d[2]
            cosine = along * inverse
            cosine_over = cosine * inverse
            theta = WAVE_SCALE * (square * inverse)
            t = theta * theta
            c1 = 1.0 + t * (-1 / 2 + t * (1 / 24 + t * (-1 / 720 + t * (1 / 40320))))
            s1 = theta * (1.0 + t * (-1 / 6 + t * (1 / 120 + t * (-1 / 5040 + t * (1 / 362880)))))
            c, s = c1, s1
            for _ in range(4):
                c, s = 1.0 - 2.0 * (s * s), 2.0 * (s * c)
            c32, s32 = 1.0 - 2.0 * (s * s), 2.0 * (s * c)
            ca, sa = jnp.where(odd, c, 1.0), jnp.where(odd, s, 0.0)
            cb, sb = jnp.where(high, c32, 1.0), jnp.where(high, s32, 0.0)
            before_re = inverse * (ca * cb - sa * sb)
            before_im = -inverse * (sa * cb + ca * sb)
            now_re = before_re * c1 + before_im * s1
            now_im = before_im * c1 - before_re * s1
            twice = 2.0 * c1
            for f in range(GROUP):
                a_re = row(Q_RE + f) + cosine * row(L_RE + f) + cosine_over * row(M_RE + f)
                a_im = row(Q_IM + f) + cosine * row(L_IM + f) + cosine_over * row(M_IM + f)
                total[f, here, :] += now_re * a_re - now_im * a_im
                total[GROUP + f, here, :] += now_re * a_im + now_im * a_re
                if f + 1 < GROUP:
                    before_re, now_re = now_re, twice * now_re - before_re
                    before_im, now_im = now_im, twice * now_im - before_im
            return inner

        return lax.fori_loop(0, OBS_HERE // BLOCK, block, carry)

    lax.fori_loop(0, groups, panels, 0)

    ones = jnp.ones((LANES, LANES), jnp.bfloat16)
    diagonal = lax.broadcasted_iota(jnp.int32, (OBS_HERE, LANES), 0) == lax.broadcasted_iota(
        jnp.int32, (OBS_HERE, LANES), 1
    )

    for i in range(ROWS):
        x = total[i]
        summed = jnp.zeros((OBS_HERE, LANES), jnp.float32)
        for _ in range(3):
            piece = x.astype(jnp.bfloat16)
            x = x - piece.astype(jnp.float32)
            summed += jnp.dot(piece, ones, preferred_element_type=jnp.float32)
        final[pl.ds(i, 1), :] = jnp.sum(jnp.where(diagonal, summed, 0.0), axis=0, keepdims=True)

    scale = wave * (1.0 / FOUR_PI)
    real = -scale * final[pl.ds(GROUP, GROUP), :]
    imag = scale * final[pl.ds(0, GROUP), :]
    for copy in range(SECTIONS):
        out[copy, pl.ds(0, GROUP), :] = real
        out[copy, pl.ds(GROUP, GROUP), :] = imag


def field(observers, tiles):
    whole = pl.BlockSpec(memory_space=pltpu.VMEM)
    return pl.pallas_call(
        field_kernel,
        out_shape=jax.ShapeDtypeStruct((SECTIONS, ROWS, OBS_HERE), jnp.float32),
        in_specs=[whole, whole],
        out_specs=whole,
        scratch_shapes=[
            pltpu.VMEM((3, OBS_HERE, LANES), jnp.float32),
            pltpu.VMEM((SPAN, PACKED, LANES), jnp.float32),
            pltpu.VMEM((ROWS, OBS_HERE, LANES), jnp.float32),
            pltpu.VMEM((ROWS, OBS_HERE), jnp.float32),
        ],
        compiler_params=pltpu.CompilerParams(vmem_limit_bytes=VMEM),
    )(observers, tiles)


def swap(x, flip):
    return lax.ppermute(x, "obs", [(i, i ^ flip) for i in range(PARTS)])


def body(series, positions, normals, areas, counts, observers):
    keep, send, geometry = spectrum_parts(series, positions, normals, areas, counts)
    pair = keep + swap(send, 1)
    sources = pair[:ROWS] + swap(pair[ROWS:], 3)
    chunk = jnp.concatenate([sources, geometry])
    tiles = lax.all_to_all(
        jnp.broadcast_to(chunk[None], (RUN, CHUNK, LANES)),
        "blk", 0, 0, tiled=True, axis_index_groups=ALONG_Z,
    )
    tiles = lax.all_to_all(
        jnp.broadcast_to(tiles[None], (LINES, RUN, CHUNK, LANES)).reshape(TILES_HERE, CHUNK, LANES),
        "blk", 0, 0, tiled=True, axis_index_groups=ALONG_X,
    )
    parts = lax.all_to_all(field(observers, tiles), "sect", 0, 0, tiled=True)
    return jnp.sum(parts, axis=0).reshape(2, GROUP, OBS_HERE)


def solution(mesh):
    placed = (
        P(None, ("sect", "blk"), "obs"),
        P(None, ("sect", "blk")),
        P(None, ("sect", "blk")),
        P(("sect", "blk")),
        P(("sect", "blk")),
        P(None, "blk"),
    )
    return jax.shard_map(
        body, mesh=mesh, in_specs=placed, out_specs=P(None, "obs", "blk"), check_vma=False
    )
```

```python
import math

import jax
import jax.numpy as jnp
import numpy as np
from jax import lax
from jax.experimental import pallas as pl
from jax.experimental.pallas import tpu as pltpu
from jax.sharding import PartitionSpec as P

SAMPLES = 512
FREQS = 64
P_DEV = 64
WAVE_SCALE = 0.05
FOUR_PI = 4.0 * math.pi

PARTS = 4
GROUP = FREQS // PARTS
ROWS = 2 * GROUP
STEPS = SAMPLES // PARTS
RUN = 8
LINES = 4
TILES_HERE = RUN * LINES
CHUNK = ROWS + 8
SECTIONS = 8
LANES = 128
OBS_HERE = 128
VMEM = 48 * 1024 * 1024

ALONG_Z = [[x * RUN + z for z in range(RUN)] for x in range(LINES)]
ALONG_X = [[x * RUN + z for x in range(LINES)] for z in range(RUN)]


def transform_rows():
    out = np.zeros((PARTS, PARTS, ROWS, STEPS), np.float64)
    for part in range(PARTS):
        steps = part * STEPS + np.arange(STEPS)
        for group in range(PARTS):
            bins = group * GROUP + 1 + np.arange(GROUP)
            angle = 2.0 * np.pi * ((bins[:, None] * steps[None, :]) % SAMPLES) / SAMPLES
            out[part, group, :GROUP] = np.cos(angle)
            out[part, group, GROUP:] = -np.sin(angle)
    return (out * SAMPLES**-0.5).astype(np.float32)


def spectrum_kernel(counts, all_rows, series, positions, normals, areas, keep, send, *scratch):
    me = lax.axis_index("obs")
    rows, samples, centres, vectors, sizes, sems = scratch
    copies = [
        pltpu.make_async_copy(source, target, sems.at[i])
        for i, (source, target) in enumerate(
            (
                (all_rows.at[me], rows),
                (series, samples),
                (areas, sizes),
                (positions, centres),
                (normals, vectors),
            )
        )
    ]
    for copy in copies:
        copy.start()
    for copy in copies:
        copy.wait()
    live = lax.broadcasted_iota(jnp.int32, (1, P_DEV), 1) < counts[0]
    weights = sizes[...] * live.astype(jnp.float32)
    weights = jnp.concatenate([weights, weights], axis=1)
    flat = samples[...].reshape(2 * P_DEV, STEPS)
    for slot, flip in enumerate((1, 2, 0, 3)):
        spectra = lax.dot_general(
            rows[me ^ flip],
            flat,
            (((1,), (1,)), ((), ())),
            precision=lax.Precision.HIGHEST,
            preferred_element_type=jnp.float32,
        )
        target = send if slot < 2 else keep
        target[pl.ds((slot % 2) * ROWS, ROWS), :] = spectra * weights
    keep[pl.ds(2 * ROWS, 8), :] = jnp.broadcast_to(counts[0].astype(jnp.float32), (8, LANES))
    keep[pl.ds(2 * ROWS, 3), :] = jnp.concatenate([centres[...], vectors[...]], axis=1)


def spectrum_parts(series, positions, normals, areas, counts):
    whole = pl.BlockSpec(memory_space=pltpu.VMEM)
    return pl.pallas_call(
        spectrum_kernel,
        out_shape=(
            jax.ShapeDtypeStruct((2 * ROWS + 8, LANES), jnp.float32),
            jax.ShapeDtypeStruct((2 * ROWS, LANES), jnp.float32),
        ),
        in_specs=[pl.BlockSpec(memory_space=pltpu.SMEM)] + [pl.BlockSpec(memory_space=pltpu.HBM)] * 5,
        out_specs=(whole,) * 2,
        scratch_shapes=[
            pltpu.VMEM((PARTS, ROWS, STEPS), jnp.float32),
            pltpu.VMEM((2, P_DEV, STEPS), jnp.float32),
            pltpu.VMEM((3, P_DEV), jnp.float32),
            pltpu.VMEM((3, P_DEV), jnp.float32),
            pltpu.VMEM((1, P_DEV), jnp.float32),
            pltpu.SemaphoreType.DMA((5,)),
        ],
        compiler_params=pltpu.CompilerParams(vmem_limit_bytes=60 * 1024 * 1024),
    )(counts, jnp.asarray(transform_rows()), series, positions, normals, areas[None])


BLOCK = 32
SPAN = TILES_HERE * P_DEV // LANES + 1
Q_RE, Q_IM, POS = 0, GROUP, ROWS
L_RE, L_IM, NORMAL = CHUNK, CHUNK + GROUP, CHUNK + ROWS
M_RE, M_IM = 2 * CHUNK, 2 * CHUNK + GROUP
PACKED = 2 * CHUNK + ROWS


def field_kernel(observers, tiles, out, spread, packed, total, final):
    group = lax.axis_index("obs")
    lane = lax.broadcasted_iota(jnp.int32, (CHUNK, LANES), 1)
    first_half = lane < P_DEV

    counts = [
        tiles[tile, pl.ds(ROWS + 3, 1), pl.ds(0, 1)][0, 0].astype(jnp.int32)
        for tile in range(TILES_HERE)
    ]
    live = jnp.int32(0)
    for tile in range(TILES_HERE):
        x = tiles[tile]
        shift, base = live & (LANES - 1), live >> 7
        ahead = lane >= shift
        for start, x_half, turn in (
            (0, jnp.where(first_half, x, 0.0), shift),
            (CHUNK, jnp.where(first_half, 0.0, x), (shift + P_DEV) & (LANES - 1)),
        ):
            turned = pltpu.roll(x_half, turn, 1)
            here = pl.ds(start, CHUNK)
            packed[base, here, :] = jnp.where(ahead, turned, packed[base, here, :])
            packed[base + 1, here, :] = jnp.where(ahead, 0.0, turned)
        live = live + counts[tile]
    groups = (live + (LANES - 1)) >> 7

    columns = jnp.transpose(
        jnp.concatenate([observers[...], jnp.zeros((LANES - 3, OBS_HERE), jnp.float32)], axis=0)
    )
    for axis in range(3):
        spread[axis] = jnp.broadcast_to(columns[:, axis : axis + 1], (OBS_HERE, LANES))

    for row in range(ROWS):
        total[row] = jnp.zeros((OBS_HERE, LANES), jnp.float32)

    numbers = group * GROUP + 1 + lax.broadcasted_iota(jnp.int32, (GROUP, LANES), 0)
    wave = WAVE_SCALE * numbers.astype(jnp.float32)
    odd, high = (group & 1) == 1, (group & 2) == 2

    def panels(at, carry):
        packed[at, pl.ds(M_RE, GROUP), :] = packed[at, pl.ds(L_IM, GROUP), :] / wave
        packed[at, pl.ds(M_IM, GROUP), :] = -packed[at, pl.ds(L_RE, GROUP), :] / wave

        def row(number):
            return jnp.broadcast_to(packed[at, pl.ds(number, 1), :], (BLOCK, LANES))

        def block(step, inner):
            here = pl.ds(pl.multiple_of(step * BLOCK, BLOCK), BLOCK)
            d = [spread[axis, here, :] - row(POS + axis) for axis in range(3)]
            square = d[0] * d[0] + d[1] * d[1] + d[2] * d[2]
            inverse = lax.rsqrt(square)
            inverse = inverse * (1.5 - 0.5 * square * inverse * inverse)
            along = row(NORMAL) * d[0] + row(NORMAL + 1) * d[1] + row(NORMAL + 2) * d[2]
            cosine = along * inverse
            cosine_over = cosine * inverse
            theta = WAVE_SCALE * (square * inverse)
            t = theta * theta
            c1 = 1.0 + t * (-1 / 2 + t * (1 / 24 + t * (-1 / 720 + t * (1 / 40320))))
            s1 = theta * (1.0 + t * (-1 / 6 + t * (1 / 120 + t * (-1 / 5040 + t * (1 / 362880)))))
            c, s = c1, s1
            for _ in range(4):
                c, s = 1.0 - 2.0 * (s * s), 2.0 * (s * c)
            c32, s32 = 1.0 - 2.0 * (s * s), 2.0 * (s * c)
            ca, sa = jnp.where(odd, c, 1.0), jnp.where(odd, s, 0.0)
            cb, sb = jnp.where(high, c32, 1.0), jnp.where(high, s32, 0.0)
            before_re = inverse * (ca * cb - sa * sb)
            before_im = -inverse * (sa * cb + ca * sb)
            now_re = before_re * c1 + before_im * s1
            now_im = before_im * c1 - before_re * s1
            twice = 2.0 * c1
            for f in range(GROUP):
                a_re = row(Q_RE + f) + cosine * row(L_RE + f) + cosine_over * row(M_RE + f)
                a_im = row(Q_IM + f) + cosine * row(L_IM + f) + cosine_over * row(M_IM + f)
                total[f, here, :] += now_re * a_re - now_im * a_im
                total[GROUP + f, here, :] += now_re * a_im + now_im * a_re
                if f + 1 < GROUP:
                    before_re, now_re = now_re, twice * now_re - before_re
                    before_im, now_im = now_im, twice * now_im - before_im
            return inner

        return lax.fori_loop(0, OBS_HERE // BLOCK, block, carry)

    lax.fori_loop(0, groups, panels, 0)

    ones = jnp.ones((LANES, LANES), jnp.bfloat16)
    diagonal = lax.broadcasted_iota(jnp.int32, (OBS_HERE, LANES), 0) == lax.broadcasted_iota(
        jnp.int32, (OBS_HERE, LANES), 1
    )

    for i in range(ROWS):
        x = total[i]
        summed = jnp.zeros((OBS_HERE, LANES), jnp.float32)
        for _ in range(2):
            piece = x.astype(jnp.bfloat16)
            x = x - piece.astype(jnp.float32)
            summed += jnp.dot(piece, ones, preferred_element_type=jnp.float32)
        final[pl.ds(i, 1), :] = jnp.sum(jnp.where(diagonal, summed, 0.0), axis=0, keepdims=True)

    scale = wave * (1.0 / FOUR_PI)
    real = -scale * final[pl.ds(GROUP, GROUP), :]
    imag = scale * final[pl.ds(0, GROUP), :]
    for copy in range(SECTIONS):
        out[copy, pl.ds(0, GROUP), :] = real
        out[copy, pl.ds(GROUP, GROUP), :] = imag


def field(observers, tiles):
    whole = pl.BlockSpec(memory_space=pltpu.VMEM)
    return pl.pallas_call(
        field_kernel,
        out_shape=jax.ShapeDtypeStruct((SECTIONS, ROWS, OBS_HERE), jnp.float32),
        in_specs=[whole, whole],
        out_specs=whole,
        scratch_shapes=[
            pltpu.VMEM((3, OBS_HERE, LANES), jnp.float32),
            pltpu.VMEM((SPAN, PACKED, LANES), jnp.float32),
            pltpu.VMEM((ROWS, OBS_HERE, LANES), jnp.float32),
            pltpu.VMEM((ROWS, OBS_HERE), jnp.float32),
        ],
        compiler_params=pltpu.CompilerParams(vmem_limit_bytes=VMEM),
    )(observers, tiles)


def from_partner(x, pairs, place):
    both = lax.all_gather(x, "obs", axis=0, axis_index_groups=pairs)
    return jnp.where(place == 0, both[1], both[0])


def body(series, positions, normals, areas, counts, observers):
    me = lax.axis_index("obs")
    keep, send = spectrum_parts(series, positions, normals, areas, counts)
    pair = keep[: 2 * ROWS] + from_partner(send, [[0, 1], [2, 3]], me & 1)
    sources = pair[:ROWS] + from_partner(pair[ROWS:], [[0, 3], [1, 2]], me >> 1)
    chunk = jnp.concatenate([sources, keep[2 * ROWS :]])
    tiles = lax.all_to_all(
        jnp.broadcast_to(chunk[None], (RUN, CHUNK, LANES)),
        "blk", 0, 0, tiled=True, axis_index_groups=ALONG_Z,
    )
    tiles = lax.all_to_all(
        jnp.broadcast_to(tiles[None], (LINES, RUN, CHUNK, LANES)).reshape(TILES_HERE, CHUNK, LANES),
        "blk", 0, 0, tiled=True, axis_index_groups=ALONG_X,
    )
    parts = lax.all_to_all(field(observers, tiles), "sect", 0, 0, tiled=True)
    return jnp.sum(parts, axis=0).reshape(2, GROUP, OBS_HERE)


def solution(mesh):
    placed = (
        P(None, ("sect", "blk"), "obs"),
        P(None, ("sect", "blk")),
        P(None, ("sect", "blk")),
        P(("sect", "blk")),
        P(("sect", "blk")),
        P(None, "blk"),
    )
    return jax.shard_map(
        body, mesh=mesh, in_specs=placed, out_specs=P(None, "obs", "blk"), check_vma=False
    )
```

```python
import math

import jax
import jax.numpy as jnp
import numpy as np
from jax import lax
from jax.experimental import pallas as pl
from jax.experimental.pallas import tpu as pltpu
from jax.sharding import PartitionSpec as P

SAMPLES = 512
FREQS = 64
P_DEV = 64
WAVE_SCALE = 0.05
FOUR_PI = 4.0 * math.pi

PARTS = 4
GROUP = FREQS // PARTS
ROWS = 2 * GROUP
STEPS = SAMPLES // PARTS
RUN = 8
LINES = 4
TILES_HERE = RUN * LINES
CHUNK = ROWS + 8
SECTIONS = 8
LANES = 128
OBS_HERE = 128
VMEM = 48 * 1024 * 1024

ALONG_Z = [[x * RUN + z for z in range(RUN)] for x in range(LINES)]
ALONG_X = [[x * RUN + z for x in range(LINES)] for z in range(RUN)]


def transform_rows():
    out = np.zeros((PARTS, PARTS, ROWS, STEPS), np.float64)
    for part in range(PARTS):
        steps = part * STEPS + np.arange(STEPS)
        for group in range(PARTS):
            bins = group * GROUP + 1 + np.arange(GROUP)
            angle = 2.0 * np.pi * ((bins[:, None] * steps[None, :]) % SAMPLES) / SAMPLES
            out[part, group, :GROUP] = np.cos(angle)
            out[part, group, GROUP:] = -np.sin(angle)
    return (out * SAMPLES**-0.5).astype(np.float32)


def spectrum_kernel(counts, all_rows, series, positions, normals, areas, keep, send, geometry, *scratch):
    me = lax.axis_index("obs")
    rows, samples, centres, vectors, sizes, sems = scratch
    copies = [
        pltpu.make_async_copy(source, target, sems.at[i])
        for i, (source, target) in enumerate(
            (
                (all_rows.at[me], rows),
                (series, samples),
                (areas, sizes),
                (positions, centres),
                (normals, vectors),
            )
        )
    ]
    for copy in copies:
        copy.start()
    for copy in copies:
        copy.wait()
    live = lax.broadcasted_iota(jnp.int32, (1, P_DEV), 1) < counts[0]
    weights = sizes[...] * live.astype(jnp.float32)
    weights = jnp.concatenate([weights, weights], axis=1)
    flat = samples[...].reshape(2 * P_DEV, STEPS)
    for slot, flip in enumerate((1, 2, 0, 3)):
        spectra = lax.dot_general(
            rows[me ^ flip],
            flat,
            (((1,), (1,)), ((), ())),
            precision=lax.Precision.HIGHEST,
            preferred_element_type=jnp.float32,
        )
        target = send if slot < 2 else keep
        target[pl.ds((slot % 2) * ROWS, ROWS), :] = spectra * weights
    geometry[...] = jnp.broadcast_to(counts[0].astype(jnp.float32), (8, LANES))
    geometry[pl.ds(0, 3), :] = jnp.concatenate([centres[...], vectors[...]], axis=1)


def spectrum_parts(series, positions, normals, areas, counts):
    block = jax.ShapeDtypeStruct((2 * ROWS, LANES), jnp.float32)
    whole = pl.BlockSpec(memory_space=pltpu.VMEM)
    return pl.pallas_call(
        spectrum_kernel,
        out_shape=(block, block, jax.ShapeDtypeStruct((8, LANES), jnp.float32)),
        in_specs=[pl.BlockSpec(memory_space=pltpu.SMEM)] + [pl.BlockSpec(memory_space=pltpu.HBM)] * 5,
        out_specs=(whole,) * 3,
        scratch_shapes=[
            pltpu.VMEM((PARTS, ROWS, STEPS), jnp.float32),
            pltpu.VMEM((2, P_DEV, STEPS), jnp.float32),
            pltpu.VMEM((3, P_DEV), jnp.float32),
            pltpu.VMEM((3, P_DEV), jnp.float32),
            pltpu.VMEM((1, P_DEV), jnp.float32),
            pltpu.SemaphoreType.DMA((5,)),
        ],
        compiler_params=pltpu.CompilerParams(vmem_limit_bytes=55091 * 1024),
    )(counts, jnp.asarray(transform_rows()), series, positions, normals, areas[None])


BLOCK = 32
SPAN = TILES_HERE * P_DEV // LANES + 1
Q_RE, Q_IM, POS = 0, GROUP, ROWS
L_RE, L_IM, NORMAL = CHUNK, CHUNK + GROUP, CHUNK + ROWS
M_RE, M_IM = 2 * CHUNK, 2 * CHUNK + GROUP
PACKED = 2 * CHUNK + ROWS


def field_kernel(observers, tiles, out, spread, packed, total, final):
    group = lax.axis_index("obs")
    lane = lax.broadcasted_iota(jnp.int32, (CHUNK, LANES), 1)
    first_half = lane < P_DEV

    counts = [
        tiles[tile, pl.ds(ROWS + 3, 1), pl.ds(0, 1)][0, 0].astype(jnp.int32)
        for tile in range(TILES_HERE)
    ]
    live = jnp.int32(0)
    for tile in range(TILES_HERE):
        x = tiles[tile]
        shift, base = live & (LANES - 1), live >> 7
        ahead = lane >= shift
        for start, x_half, turn in (
            (0, jnp.where(first_half, x, 0.0), shift),
            (CHUNK, jnp.where(first_half, 0.0, x), (shift + P_DEV) & (LANES - 1)),
        ):
            turned = pltpu.roll(x_half, turn, 1)
            here = pl.ds(start, CHUNK)
            packed[base, here, :] = jnp.where(ahead, turned, packed[base, here, :])
            packed[base + 1, here, :] = jnp.where(ahead, 0.0, turned)
        live = live + counts[tile]
    groups = (live + (LANES - 1)) >> 7

    columns = jnp.transpose(
        jnp.concatenate([observers[...], jnp.zeros((LANES - 3, OBS_HERE), jnp.float32)], axis=0)
    )
    for axis in range(3):
        spread[axis] = jnp.broadcast_to(columns[:, axis : axis + 1], (OBS_HERE, LANES))

    for row in range(ROWS):
        total[row] = jnp.zeros((OBS_HERE, LANES), jnp.float32)

    numbers = group * GROUP + 1 + lax.broadcasted_iota(jnp.int32, (GROUP, LANES), 0)
    wave = WAVE_SCALE * numbers.astype(jnp.float32)
    odd, high = (group & 1) == 1, (group & 2) == 2

    def panels(at, carry):
        packed[at, pl.ds(M_RE, GROUP), :] = packed[at, pl.ds(L_IM, GROUP), :] / wave
        packed[at, pl.ds(M_IM, GROUP), :] = -packed[at, pl.ds(L_RE, GROUP), :] / wave

        def row(number):
            return jnp.broadcast_to(packed[at, pl.ds(number, 1), :], (BLOCK, LANES))

        def block(step, inner):
            here = pl.ds(pl.multiple_of(step * BLOCK, BLOCK), BLOCK)
            d = [spread[axis, here, :] - row(POS + axis) for axis in range(3)]
            square = d[0] * d[0] + d[1] * d[1] + d[2] * d[2]
            inverse = lax.rsqrt(square)
            along = row(NORMAL) * d[0] + row(NORMAL + 1) * d[1] + row(NORMAL + 2) * d[2]
            cosine = along * inverse
            cosine_over = cosine * inverse
            theta = WAVE_SCALE * (square * inverse)
            t = theta * theta
            c1 = 1.0 + t * (-1 / 2 + t * (1 / 24 + t * (-1 / 720 + t * (1 / 40320))))
            s1 = theta * (1.0 + t * (-1 / 6 + t * (1 / 120 + t * (-1 / 5040 + t * (1 / 362880)))))
            c, s = c1, s1
            for _ in range(4):
                c, s = 1.0 - 2.0 * (s * s), 2.0 * (s * c)
            c32, s32 = 1.0 - 2.0 * (s * s), 2.0 * (s * c)
            ca, sa = jnp.where(odd, c, 1.0), jnp.where(odd, s, 0.0)
            cb, sb = jnp.where(high, c32, 1.0), jnp.where(high, s32, 0.0)
            before_re = inverse * (ca * cb - sa * sb)
            before_im = -inverse * (sa * cb + ca * sb)
            now_re = before_re * c1 + before_im * s1
            now_im = before_im * c1 - before_re * s1
            twice = 2.0 * c1
            for f in range(GROUP):
                a_re = row(Q_RE + f) + cosine * row(L_RE + f) + cosine_over * row(M_RE + f)
                a_im = row(Q_IM + f) + cosine * row(L_IM + f) + cosine_over * row(M_IM + f)
                total[f, here, :] += now_re * a_re - now_im * a_im
                total[GROUP + f, here, :] += now_re * a_im + now_im * a_re
                if f + 1 < GROUP:
                    before_re, now_re = now_re, twice * now_re - before_re
                    before_im, now_im = now_im, twice * now_im - before_im
            return inner

        return lax.fori_loop(0, OBS_HERE // BLOCK, block, carry)

    lax.fori_loop(0, groups, panels, 0)

    ones = jnp.ones((LANES, LANES), jnp.bfloat16)
    diagonal = lax.broadcasted_iota(jnp.int32, (OBS_HERE, LANES), 0) == lax.broadcasted_iota(
        jnp.int32, (OBS_HERE, LANES), 1
    )

    for i in range(ROWS):
        x = total[i]
        summed = jnp.zeros((OBS_HERE, LANES), jnp.float32)
        for _ in range(2):
            piece = x.astype(jnp.bfloat16)
            x = x - piece.astype(jnp.float32)
            summed += jnp.dot(piece, ones, preferred_element_type=jnp.float32)
        final[pl.ds(i, 1), :] = jnp.sum(jnp.where(diagonal, summed, 0.0), axis=0, keepdims=True)

    scale = wave * (1.0 / FOUR_PI)
    real = -scale * final[pl.ds(GROUP, GROUP), :]
    imag = scale * final[pl.ds(0, GROUP), :]
    for copy in range(SECTIONS):
        out[copy, pl.ds(0, GROUP), :] = real
        out[copy, pl.ds(GROUP, GROUP), :] = imag


def field(observers, tiles):
    whole = pl.BlockSpec(memory_space=pltpu.VMEM)
    return pl.pallas_call(
        field_kernel,
        out_shape=jax.ShapeDtypeStruct((SECTIONS, ROWS, OBS_HERE), jnp.float32),
        in_specs=[whole, whole],
        out_specs=whole,
        scratch_shapes=[
            pltpu.VMEM((3, OBS_HERE, LANES), jnp.float32),
            pltpu.VMEM((SPAN, PACKED, LANES), jnp.float32),
            pltpu.VMEM((ROWS, OBS_HERE, LANES), jnp.float32),
            pltpu.VMEM((ROWS, OBS_HERE), jnp.float32),
        ],
        compiler_params=pltpu.CompilerParams(vmem_limit_bytes=VMEM),
    )(observers, tiles)


def from_partner(x, pairs, place):
    both = lax.all_gather(x, "obs", axis=0, axis_index_groups=pairs)
    return jnp.where(place == 0, both[1], both[0])


def body(series, positions, normals, areas, counts, observers):
    me = lax.axis_index("obs")
    keep, send, geometry = spectrum_parts(series, positions, normals, areas, counts)
    pair = keep + from_partner(send, [[0, 1], [2, 3]], me & 1)
    sources = pair[:ROWS] + from_partner(pair[ROWS:], [[0, 3], [1, 2]], me >> 1)
    chunk = jnp.concatenate([sources, geometry])
    tiles = lax.all_to_all(
        jnp.broadcast_to(chunk[None], (RUN, CHUNK, LANES)),
        "blk", 0, 0, tiled=True, axis_index_groups=ALONG_Z,
    )
    tiles = lax.all_to_all(
        jnp.broadcast_to(tiles[None], (LINES, RUN, CHUNK, LANES)).reshape(TILES_HERE, CHUNK, LANES),
        "blk", 0, 0, tiled=True, axis_index_groups=ALONG_X,
    )
    parts = lax.all_to_all(field(observers, tiles), "sect", 0, 0, tiled=True)
    return jnp.sum(parts, axis=0).reshape(2, GROUP, OBS_HERE)


def solution(mesh):
    placed = (
        P(None, ("sect", "blk"), "obs"),
        P(None, ("sect", "blk")),
        P(None, ("sect", "blk")),
        P(("sect", "blk")),
        P(("sect", "blk")),
        P(None, "blk"),
    )
    return jax.shard_map(
        body, mesh=mesh, in_specs=placed, out_specs=P(None, "obs", "blk"), check_vma=False
    )
```

```python
import math

import jax
import jax.numpy as jnp
import numpy as np
from jax import lax
from jax.experimental import pallas as pl
from jax.experimental.pallas import tpu as pltpu
from jax.sharding import PartitionSpec as P

SAMPLES = 512
FREQS = 64
P_DEV = 64
WAVE_SCALE = 0.05
FOUR_PI = 4.0 * math.pi

PARTS = 4
GROUP = FREQS // PARTS
ROWS = 2 * GROUP
STEPS = SAMPLES // PARTS
RUN = 8
LINES = 4
TILES_HERE = RUN * LINES
CHUNK = ROWS + 8
SECTIONS = 8
LANES = 128
OBS_HERE = 128
VMEM = 48 * 1024 * 1024

ALONG_Z = [[x * RUN + z for z in range(RUN)] for x in range(LINES)]
ALONG_X = [[x * RUN + z for x in range(LINES)] for z in range(RUN)]


def transform_rows():
    out = np.zeros((PARTS, PARTS, ROWS, STEPS), np.float64)
    for part in range(PARTS):
        steps = part * STEPS + np.arange(STEPS)
        for group in range(PARTS):
            bins = group * GROUP + 1 + np.arange(GROUP)
            angle = 2.0 * np.pi * ((bins[:, None] * steps[None, :]) % SAMPLES) / SAMPLES
            out[part, group, :GROUP] = np.cos(angle)
            out[part, group, GROUP:] = -np.sin(angle)
    return (out * SAMPLES**-0.5).astype(np.float32)


def spectrum_kernel(counts, all_rows, series, panels, keep, send, geometry, *scratch):
    me = lax.axis_index("obs")
    rows, samples, sems = scratch
    copies = [
        pltpu.make_async_copy(source, target, sems.at[i])
        for i, (source, target) in enumerate(
            (
                (all_rows.at[me], rows),
                (series, samples),
            )
        )
    ]
    for copy in copies:
        copy.start()
    for copy in copies:
        copy.wait()
    live = lax.broadcasted_iota(jnp.int32, (1, P_DEV), 1) < counts[0]
    weights = panels[pl.ds(6, 1), :] * live.astype(jnp.float32)
    weights = jnp.concatenate([weights, weights], axis=1)
    flat = samples[...].reshape(2 * P_DEV, STEPS)
    for slot, flip in enumerate((1, 2, 0, 3)):
        spectra = lax.dot_general(
            rows[me ^ flip],
            flat,
            (((1,), (1,)), ((), ())),
            precision=lax.Precision.HIGHEST,
            preferred_element_type=jnp.float32,
        )
        target = send if slot < 2 else keep
        target[pl.ds((slot % 2) * ROWS, ROWS), :] = spectra * weights
    geometry[...] = jnp.broadcast_to(counts[0].astype(jnp.float32), (8, LANES))
    geometry[pl.ds(0, 3), :] = jnp.concatenate(
        [panels[pl.ds(0, 3), :], panels[pl.ds(3, 3), :]], axis=1
    )


def spectrum_parts(series, positions, normals, areas, counts):
    block = jax.ShapeDtypeStruct((2 * ROWS, LANES), jnp.float32)
    whole = pl.BlockSpec(memory_space=pltpu.VMEM)
    panels = jnp.concatenate([positions, normals, areas[None], areas[None]])
    return pl.pallas_call(
        spectrum_kernel,
        out_shape=(block, block, jax.ShapeDtypeStruct((8, LANES), jnp.float32)),
        in_specs=[pl.BlockSpec(memory_space=pltpu.SMEM)]
        + [pl.BlockSpec(memory_space=pltpu.HBM)] * 2
        + [whole],
        out_specs=(whole,) * 3,
        scratch_shapes=[
            pltpu.VMEM((PARTS, ROWS, STEPS), jnp.float32),
            pltpu.VMEM((2, P_DEV, STEPS), jnp.float32),
            pltpu.SemaphoreType.DMA((2,)),
        ],
        compiler_params=pltpu.CompilerParams(vmem_limit_bytes=55130 * 1024),
    )(counts, jnp.asarray(transform_rows()), series, panels)


BLOCK = 32
Q_RE, Q_IM, POS = 0, GROUP, ROWS
L_RE, L_IM, NORMAL = CHUNK, CHUNK + GROUP, CHUNK + ROWS
M_RE, M_IM = 2 * CHUNK, 2 * CHUNK + GROUP
PACKED = 2 * CHUNK + ROWS


def add_tiles(observers, tiles, chosen, spread, packed, total):
    group = lax.axis_index("obs")
    lane = lax.broadcasted_iota(jnp.int32, (CHUNK, LANES), 1)
    first_half = lane < P_DEV

    counts = [
        tiles[tile, pl.ds(ROWS + 3, 1), pl.ds(0, 1)][0, 0].astype(jnp.int32) for tile in chosen
    ]
    live = jnp.int32(0)
    for tile, count in zip(chosen, counts):
        x = tiles[tile]
        shift, base = live & (LANES - 1), live >> 7
        ahead = lane >= shift
        for start, x_half, turn in (
            (0, jnp.where(first_half, x, 0.0), shift),
            (CHUNK, jnp.where(first_half, 0.0, x), (shift + P_DEV) & (LANES - 1)),
        ):
            turned = pltpu.roll(x_half, turn, 1)
            here = pl.ds(start, CHUNK)
            packed[base, here, :] = jnp.where(ahead, turned, packed[base, here, :])
            packed[base + 1, here, :] = jnp.where(ahead, 0.0, turned)
        live = live + count
    groups = (live + (LANES - 1)) >> 7

    columns = jnp.transpose(
        jnp.concatenate([observers[...], jnp.zeros((LANES - 3, OBS_HERE), jnp.float32)], axis=0)
    )
    for axis in range(3):
        spread[axis] = jnp.broadcast_to(columns[:, axis : axis + 1], (OBS_HERE, LANES))

    numbers = group * GROUP + 1 + lax.broadcasted_iota(jnp.int32, (GROUP, LANES), 0)
    wave = WAVE_SCALE * numbers.astype(jnp.float32)
    odd, high = (group & 1) == 1, (group & 2) == 2

    def panels(at, carry):
        packed[at, pl.ds(M_RE, GROUP), :] = packed[at, pl.ds(L_IM, GROUP), :] / wave
        packed[at, pl.ds(M_IM, GROUP), :] = -packed[at, pl.ds(L_RE, GROUP), :] / wave

        def row(number):
            return jnp.broadcast_to(packed[at, pl.ds(number, 1), :], (BLOCK, LANES))

        def block(step, inner):
            here = pl.ds(pl.multiple_of(step * BLOCK, BLOCK), BLOCK)
            d = [spread[axis, here, :] - row(POS + axis) for axis in range(3)]
            square = d[0] * d[0] + d[1] * d[1] + d[2] * d[2]
            inverse = lax.rsqrt(square)
            along = row(NORMAL) * d[0] + row(NORMAL + 1) * d[1] + row(NORMAL + 2) * d[2]
            cosine = along * inverse
            cosine_over = cosine * inverse
            theta = WAVE_SCALE * (square * inverse)
            t = theta * theta
            c1 = 1.0 + t * (-1 / 2 + t * (1 / 24 + t * (-1 / 720 + t * (1 / 40320))))
            s1 = theta * (1.0 + t * (-1 / 6 + t * (1 / 120 + t * (-1 / 5040 + t * (1 / 362880)))))
            c, s = c1, s1
            for _ in range(4):
                c, s = 1.0 - 2.0 * (s * s), 2.0 * (s * c)
            c32, s32 = 1.0 - 2.0 * (s * s), 2.0 * (s * c)
            ca, sa = jnp.where(odd, c, 1.0), jnp.where(odd, s, 0.0)
            cb, sb = jnp.where(high, c32, 1.0), jnp.where(high, s32, 0.0)
            before_re = inverse * (ca * cb - sa * sb)
            before_im = -inverse * (sa * cb + ca * sb)
            now_re = before_re * c1 + before_im * s1
            now_im = before_im * c1 - before_re * s1
            twice = 2.0 * c1
            for f in range(GROUP):
                a_re = row(Q_RE + f) + cosine * row(L_RE + f) + cosine_over * row(M_RE + f)
                a_im = row(Q_IM + f) + cosine * row(L_IM + f) + cosine_over * row(M_IM + f)
                total[f, here, :] += now_re * a_re - now_im * a_im
                total[GROUP + f, here, :] += now_re * a_im + now_im * a_re
                if f + 1 < GROUP:
                    before_re, now_re = now_re, twice * now_re - before_re
                    before_im, now_im = now_im, twice * now_im - before_im
            return inner

        return lax.fori_loop(0, OBS_HERE // BLOCK, block, carry)

    lax.fori_loop(0, groups, panels, 0)


def own_kernel(observers, tiles, total, spread, packed):
    for row in range(ROWS):
        total[row] = jnp.zeros((OBS_HERE, LANES), jnp.float32)
    add_tiles(observers, tiles, list(range(RUN)), spread, packed, total)


def other_kernel(observers, tiles, begun, out, spread, packed, total, final):
    line = lax.axis_index("blk") >> 3
    chosen = [
        ((line + step) & (LINES - 1)) * RUN + tile for step in range(1, LINES) for tile in range(RUN)
    ]
    for row in range(ROWS):
        total[row] = begun[row]
    add_tiles(observers, tiles, chosen, spread, packed, total)

    wave = WAVE_SCALE * (
        lax.axis_index("obs") * GROUP + 1 + lax.broadcasted_iota(jnp.int32, (GROUP, LANES), 0)
    ).astype(jnp.float32)
    ones = jnp.ones((LANES, LANES), jnp.bfloat16)
    diagonal = lax.broadcasted_iota(jnp.int32, (OBS_HERE, LANES), 0) == lax.broadcasted_iota(
        jnp.int32, (OBS_HERE, LANES), 1
    )

    for i in range(ROWS):
        x = total[i]
        summed = jnp.zeros((OBS_HERE, LANES), jnp.float32)
        for _ in range(2):
            piece = x.astype(jnp.bfloat16)
            x = x - piece.astype(jnp.float32)
            summed += jnp.dot(piece, ones, preferred_element_type=jnp.float32)
        final[pl.ds(i, 1), :] = jnp.sum(jnp.where(diagonal, summed, 0.0), axis=0, keepdims=True)

    scale = wave * (1.0 / FOUR_PI)
    real = -scale * final[pl.ds(GROUP, GROUP), :]
    imag = scale * final[pl.ds(0, GROUP), :]
    for copy in range(SECTIONS):
        out[copy, pl.ds(0, GROUP), :] = real
        out[copy, pl.ds(GROUP, GROUP), :] = imag


WHOLE = pl.BlockSpec(memory_space=pltpu.VMEM)
TOTAL = (ROWS, OBS_HERE, LANES)


def shared_scratch(tiles):
    return [
        pltpu.VMEM((3, OBS_HERE, LANES), jnp.float32),
        pltpu.VMEM((tiles * P_DEV // LANES + 1, PACKED, LANES), jnp.float32),
    ]


def field_of_own(observers, tiles):
    return pl.pallas_call(
        own_kernel,
        out_shape=jax.ShapeDtypeStruct(TOTAL, jnp.float32),
        in_specs=[WHOLE] * 2,
        out_specs=WHOLE,
        scratch_shapes=shared_scratch(RUN),
        compiler_params=pltpu.CompilerParams(vmem_limit_bytes=24 * 1024 * 1024),
        cost_estimate=pl.CostEstimate(flops=1 << 30, bytes_accessed=1 << 22, transcendentals=0),
    )(observers, tiles)


def field_of_others(observers, tiles, begun):
    return pl.pallas_call(
        other_kernel,
        out_shape=jax.ShapeDtypeStruct((SECTIONS, ROWS, OBS_HERE), jnp.float32),
        in_specs=[WHOLE] * 3,
        out_specs=WHOLE,
        scratch_shapes=shared_scratch(TILES_HERE - RUN)
        + [pltpu.VMEM(TOTAL, jnp.float32), pltpu.VMEM((ROWS, OBS_HERE), jnp.float32)],
        compiler_params=pltpu.CompilerParams(vmem_limit_bytes=24 * 1024 * 1024),
    )(observers, tiles, begun)


def from_partner(x, pairs, place):
    both = lax.all_gather(x, "obs", axis=0, axis_index_groups=pairs)
    return jnp.where(place == 0, both[1], both[0])


def body(series, positions, normals, areas, counts, observers):
    me = lax.axis_index("obs")
    keep, send, geometry = spectrum_parts(series, positions, normals, areas, counts)
    pair = keep + from_partner(send, [[0, 1], [2, 3]], me & 1)
    sources = pair[:ROWS] + from_partner(pair[ROWS:], [[0, 3], [1, 2]], me >> 1)
    chunk = jnp.concatenate([sources, geometry])
    own = lax.all_to_all(
        jnp.broadcast_to(chunk[None], (RUN, CHUNK, LANES)),
        "blk", 0, 0, tiled=True, axis_index_groups=ALONG_Z,
    )
    tiles = lax.all_to_all(
        jnp.broadcast_to(own[None], (LINES, RUN, CHUNK, LANES)).reshape(TILES_HERE, CHUNK, LANES),
        "blk", 0, 0, tiled=True, axis_index_groups=ALONG_X,
    )
    begun = field_of_own(observers, own)
    parts = lax.all_to_all(field_of_others(observers, tiles, begun), "sect", 0, 0, tiled=True)
    return jnp.sum(parts, axis=0).reshape(2, GROUP, OBS_HERE)


def solution(mesh):
    placed = (
        P(None, ("sect", "blk"), "obs"),
        P(None, ("sect", "blk")),
        P(None, ("sect", "blk")),
        P(("sect", "blk")),
        P(("sect", "blk")),
        P(None, "blk"),
    )
    return jax.shard_map(
        body, mesh=mesh, in_specs=placed, out_specs=P(None, "obs", "blk"), check_vma=False
    )
```

```python
import math

import jax
import jax.numpy as jnp
import numpy as np
from jax import lax
from jax.experimental import pallas as pl
from jax.experimental.pallas import tpu as pltpu
from jax.sharding import PartitionSpec as P

SAMPLES = 512
FREQS = 64
P_DEV = 64
WAVE_SCALE = 0.05
FOUR_PI = 4.0 * math.pi

PARTS = 4
GROUP = FREQS // PARTS
ROWS = 2 * GROUP
STEPS = SAMPLES // PARTS
RUN = 8
LINES = 4
TILES_HERE = RUN * LINES
CHUNK = ROWS + 8
SECTIONS = 8
LANES = 128
OBS_HERE = 128
VMEM = 48 * 1024 * 1024

ALONG_Z = [[x * RUN + z for z in range(RUN)] for x in range(LINES)]
ALONG_X = [[x * RUN + z for x in range(LINES)] for z in range(RUN)]


def transform_rows():
    out = np.zeros((PARTS, PARTS, ROWS, STEPS), np.float64)
    for part in range(PARTS):
        steps = part * STEPS + np.arange(STEPS)
        for group in range(PARTS):
            bins = group * GROUP + 1 + np.arange(GROUP)
            angle = 2.0 * np.pi * ((bins[:, None] * steps[None, :]) % SAMPLES) / SAMPLES
            out[part, group, :GROUP] = np.cos(angle)
            out[part, group, GROUP:] = -np.sin(angle)
    return (out * SAMPLES**-0.5).astype(np.float32)


def spectrum_kernel(counts, all_rows, series, panels, keep, send, geometry, *scratch):
    me = lax.axis_index("obs")
    rows, samples, sems = scratch
    copies = [
        pltpu.make_async_copy(source, target, sems.at[i])
        for i, (source, target) in enumerate(
            (
                (all_rows.at[me], rows),
                (series, samples),
            )
        )
    ]
    for copy in copies:
        copy.start()
    for copy in copies:
        copy.wait()
    live = lax.broadcasted_iota(jnp.int32, (1, P_DEV), 1) < counts[0]
    weights = panels[pl.ds(6, 1), :] * live.astype(jnp.float32)
    weights = jnp.concatenate([weights, weights], axis=1)
    flat = samples[...].reshape(2 * P_DEV, STEPS)
    for slot, flip in enumerate((1, 2, 0, 3)):
        spectra = lax.dot_general(
            rows[me ^ flip],
            flat,
            (((1,), (1,)), ((), ())),
            precision=lax.Precision.HIGHEST,
            preferred_element_type=jnp.float32,
        )
        target = send if slot < 2 else keep
        target[pl.ds((slot % 2) * ROWS, ROWS), :] = spectra * weights
    geometry[...] = jnp.broadcast_to(counts[0].astype(jnp.float32), (8, LANES))
    geometry[pl.ds(0, 3), :] = jnp.concatenate(
        [panels[pl.ds(0, 3), :], panels[pl.ds(3, 3), :]], axis=1
    )


def spectrum_parts(series, positions, normals, areas, counts):
    block = jax.ShapeDtypeStruct((2 * ROWS, LANES), jnp.float32)
    whole = pl.BlockSpec(memory_space=pltpu.VMEM)
    panels = jnp.concatenate([positions, normals, areas[None], areas[None]])
    return pl.pallas_call(
        spectrum_kernel,
        out_shape=(block, block, jax.ShapeDtypeStruct((8, LANES), jnp.float32)),
        in_specs=[pl.BlockSpec(memory_space=pltpu.SMEM)]
        + [pl.BlockSpec(memory_space=pltpu.HBM)] * 2
        + [whole],
        out_specs=(whole,) * 3,
        scratch_shapes=[
            pltpu.VMEM((PARTS, ROWS, STEPS), jnp.float32),
            pltpu.VMEM((2, P_DEV, STEPS), jnp.float32),
            pltpu.SemaphoreType.DMA((2,)),
        ],
        compiler_params=pltpu.CompilerParams(vmem_limit_bytes=55130 * 1024),
    )(counts, jnp.asarray(transform_rows()), series, panels)


BLOCK = 32
Q_RE, Q_IM, POS = 0, GROUP, ROWS
L_RE, L_IM, NORMAL = CHUNK, CHUNK + GROUP, CHUNK + ROWS
M_RE, M_IM = 2 * CHUNK, 2 * CHUNK + GROUP
PACKED = 2 * CHUNK + ROWS


def add_tiles(tiles, chosen, spread, packed, total):
    group = lax.axis_index("obs")
    lane = lax.broadcasted_iota(jnp.int32, (CHUNK, LANES), 1)
    first_half = lane < P_DEV

    counts = [
        tiles[tile, pl.ds(ROWS + 3, 1), pl.ds(0, 1)][0, 0].astype(jnp.int32) for tile in chosen
    ]
    live = jnp.int32(0)
    for tile, count in zip(chosen, counts):
        x = tiles[tile]
        shift, base = live & (LANES - 1), live >> 7
        ahead = lane >= shift
        for start, x_half, turn in (
            (0, jnp.where(first_half, x, 0.0), shift),
            (CHUNK, jnp.where(first_half, 0.0, x), (shift + P_DEV) & (LANES - 1)),
        ):
            turned = pltpu.roll(x_half, turn, 1)
            here = pl.ds(start, CHUNK)
            packed[base, here, :] = jnp.where(ahead, turned, packed[base, here, :])
            packed[base + 1, here, :] = jnp.where(ahead, 0.0, turned)
        live = live + count
    groups = (live + (LANES - 1)) >> 7

    numbers = group * GROUP + 1 + lax.broadcasted_iota(jnp.int32, (GROUP, LANES), 0)
    wave = WAVE_SCALE * numbers.astype(jnp.float32)
    odd, high = (group & 1) == 1, (group & 2) == 2

    def panels(at, carry):
        packed[at, pl.ds(M_RE, GROUP), :] = packed[at, pl.ds(L_IM, GROUP), :] / wave
        packed[at, pl.ds(M_IM, GROUP), :] = -packed[at, pl.ds(L_RE, GROUP), :] / wave

        def row(number):
            return jnp.broadcast_to(packed[at, pl.ds(number, 1), :], (BLOCK, LANES))

        def block(step, inner):
            here = pl.ds(pl.multiple_of(step * BLOCK, BLOCK), BLOCK)
            d = [spread[axis, here, :] - row(POS + axis) for axis in range(3)]
            square = d[0] * d[0] + d[1] * d[1] + d[2] * d[2]
            inverse = lax.rsqrt(square)
            along = row(NORMAL) * d[0] + row(NORMAL + 1) * d[1] + row(NORMAL + 2) * d[2]
            cosine = along * inverse
            cosine_over = cosine * inverse
            theta = WAVE_SCALE * (square * inverse)
            t = theta * theta
            c1 = 1.0 + t * (-1 / 2 + t * (1 / 24 + t * (-1 / 720 + t * (1 / 40320))))
            s1 = theta * (1.0 + t * (-1 / 6 + t * (1 / 120 + t * (-1 / 5040 + t * (1 / 362880)))))
            c, s = c1, s1
            for _ in range(4):
                c, s = 1.0 - 2.0 * (s * s), 2.0 * (s * c)
            c32, s32 = 1.0 - 2.0 * (s * s), 2.0 * (s * c)
            ca, sa = jnp.where(odd, c, 1.0), jnp.where(odd, s, 0.0)
            cb, sb = jnp.where(high, c32, 1.0), jnp.where(high, s32, 0.0)
            before_re = inverse * (ca * cb - sa * sb)
            before_im = -inverse * (sa * cb + ca * sb)
            now_re = before_re * c1 + before_im * s1
            now_im = before_im * c1 - before_re * s1
            twice = 2.0 * c1
            for f in range(GROUP):
                a_re = row(Q_RE + f) + cosine * row(L_RE + f) + cosine_over * row(M_RE + f)
                a_im = row(Q_IM + f) + cosine * row(L_IM + f) + cosine_over * row(M_IM + f)
                total[f, here, :] += now_re * a_re - now_im * a_im
                total[GROUP + f, here, :] += now_re * a_im + now_im * a_re
                if f + 1 < GROUP:
                    before_re, now_re = now_re, twice * now_re - before_re
                    before_im, now_im = now_im, twice * now_im - before_im
            return inner

        return lax.fori_loop(0, OBS_HERE // BLOCK, block, carry)

    lax.fori_loop(0, groups, panels, 0)


def own_kernel(observers, tiles, total, spread, packed):
    columns = jnp.transpose(
        jnp.concatenate([observers[...], jnp.zeros((LANES - 3, OBS_HERE), jnp.float32)], axis=0)
    )
    for axis in range(3):
        spread[axis] = jnp.broadcast_to(columns[:, axis : axis + 1], (OBS_HERE, LANES))

    for row in range(ROWS):
        total[row] = jnp.zeros((OBS_HERE, LANES), jnp.float32)
    add_tiles(tiles, list(range(RUN)), spread, packed, total)


def other_kernel(tiles, begun, spread, out, packed, total, final):
    line = lax.axis_index("blk") >> 3
    chosen = [
        ((line + step) & (LINES - 1)) * RUN + tile for step in range(1, LINES) for tile in range(RUN)
    ]
    for row in range(ROWS):
        total[row] = begun[row]
    add_tiles(tiles, chosen, spread, packed, total)

    wave = WAVE_SCALE * (
        lax.axis_index("obs") * GROUP + 1 + lax.broadcasted_iota(jnp.int32, (GROUP, LANES), 0)
    ).astype(jnp.float32)
    ones = jnp.ones((LANES, LANES), jnp.bfloat16)
    diagonal = lax.broadcasted_iota(jnp.int32, (OBS_HERE, LANES), 0) == lax.broadcasted_iota(
        jnp.int32, (OBS_HERE, LANES), 1
    )

    for i in range(ROWS):
        x = total[i]
        summed = jnp.zeros((OBS_HERE, LANES), jnp.float32)
        for _ in range(2):
            piece = x.astype(jnp.bfloat16)
            x = x - piece.astype(jnp.float32)
            summed += jnp.dot(piece, ones, preferred_element_type=jnp.float32)
        final[pl.ds(i, 1), :] = jnp.sum(jnp.where(diagonal, summed, 0.0), axis=0, keepdims=True)

    scale = wave * (1.0 / FOUR_PI)
    real = -scale * final[pl.ds(GROUP, GROUP), :]
    imag = scale * final[pl.ds(0, GROUP), :]
    for copy in range(SECTIONS):
        out[copy, pl.ds(0, GROUP), :] = real
        out[copy, pl.ds(GROUP, GROUP), :] = imag


WHOLE = pl.BlockSpec(memory_space=pltpu.VMEM)
TOTAL = (ROWS, OBS_HERE, LANES)


def shared_scratch(tiles):
    return [
        pltpu.VMEM((tiles * P_DEV // LANES + 1, PACKED, LANES), jnp.float32),
    ]


def field_of_own(observers, tiles):
    return pl.pallas_call(
        own_kernel,
        out_shape=(
            jax.ShapeDtypeStruct(TOTAL, jnp.float32),
            jax.ShapeDtypeStruct((3, OBS_HERE, LANES), jnp.float32),
        ),
        in_specs=[WHOLE] * 2,
        out_specs=(WHOLE,) * 2,
        scratch_shapes=shared_scratch(RUN),
        compiler_params=pltpu.CompilerParams(vmem_limit_bytes=24 * 1024 * 1024),
        cost_estimate=pl.CostEstimate(flops=1 << 30, bytes_accessed=1 << 22, transcendentals=0),
    )(observers, tiles)


def field_of_others(tiles, begun, spread):
    return pl.pallas_call(
        other_kernel,
        out_shape=jax.ShapeDtypeStruct((SECTIONS, ROWS, OBS_HERE), jnp.float32),
        in_specs=[WHOLE] * 3,
        out_specs=WHOLE,
        scratch_shapes=shared_scratch(TILES_HERE - RUN)
        + [pltpu.VMEM(TOTAL, jnp.float32), pltpu.VMEM((ROWS, OBS_HERE), jnp.float32)],
        compiler_params=pltpu.CompilerParams(vmem_limit_bytes=24 * 1024 * 1024),
    )(tiles, begun, spread)


def from_partner(x, pairs, place):
    both = lax.all_gather(x, "obs", axis=0, axis_index_groups=pairs)
    return jnp.where(place == 0, both[1], both[0])


def body(series, positions, normals, areas, counts, observers):
    me = lax.axis_index("obs")
    keep, send, geometry = spectrum_parts(series, positions, normals, areas, counts)
    pair = keep + from_partner(send, [[0, 1], [2, 3]], me & 1)
    sources = pair[:ROWS] + from_partner(pair[ROWS:], [[0, 3], [1, 2]], me >> 1)
    chunk = jnp.concatenate([sources, geometry])
    own = lax.all_to_all(
        jnp.broadcast_to(chunk[None], (RUN, CHUNK, LANES)),
        "blk", 0, 0, tiled=True, axis_index_groups=ALONG_Z,
    )
    tiles = lax.all_to_all(
        jnp.broadcast_to(own[None], (LINES, RUN, CHUNK, LANES)).reshape(TILES_HERE, CHUNK, LANES),
        "blk", 0, 0, tiled=True, axis_index_groups=ALONG_X,
    )
    begun, spread = field_of_own(observers, own)
    parts = lax.all_to_all(field_of_others(tiles, begun, spread), "sect", 0, 0, tiled=True)
    return jnp.sum(parts, axis=0).reshape(2, GROUP, OBS_HERE)


def solution(mesh):
    placed = (
        P(None, ("sect", "blk"), "obs"),
        P(None, ("sect", "blk")),
        P(None, ("sect", "blk")),
        P(("sect", "blk")),
        P(("sect", "blk")),
        P(None, "blk"),
    )
    return jax.shard_map(
        body, mesh=mesh, in_specs=placed, out_specs=P(None, "obs", "blk"), check_vma=False
    )
```
